32 devices in a mesh: dp: 4 (over z), head: 4 (over x, core), group: 2 (over y).
Axes of the slice: x: 2, y: 2, z: 4, core: 2. Of those that a mesh axis runs over, the one named last changes fastest.
Arguments:
- tokens: bfloat16 [2048, 2048], P(('dp', 'head')), may hold values from -6 to 6
- grad_out: bfloat16 [2048, 2048], P(('dp', 'head')), may hold values from -6 to 6
- w_qkv: bfloat16 [3, 2048, 1024], P(None, None, ('head', 'group')), may hold values from -4 to 4
- w_attn_out: bfloat16 [1024, 2048], P(('head', 'group')), may hold values from -0.1875 to 0.1875
- gain_attn: float32 [2048], replicated, may hold values from 0.25 to 1.75
- gain_ffn: float32 [2048], replicated, may hold values from 0.25 to 1.75
- w_gate_up: bfloat16 [16, 2, 2048, 1408], P(('dp', 'head'), None, None, 'group'), may hold values from -0.125 to 0.125
- w_down: bfloat16 [16, 1408, 2048], P(('dp', 'head'), 'group'), may hold values from -0.15625 to 0.15625
- expert_ids: int32 [2048, 2], P(('dp', 'head')), may hold values from 0 to 15, all different within a row; in each aligned block of 128 rows (0 to 127, 128 to 255, ...) at most 20 rows name the same one
- gates: float32 [2048, 2], P(('dp', 'head')), may hold values from 0.05 to 0.5
Outputs:
- grad_tokens: bfloat16 [2048, 2048], P(('dp', 'head'))
- grad_qkv: float32 [3, 2048, 1024], P(None, 'dp', ('head', 'group'))
- grad_attn_out: float32 [1024, 2048], P(('head', 'group'), 'dp')
- grad_gate_up: bfloat16 [16, 2, 2048, 1408], P(('dp', 'head'), None, None, 'group')
- grad_down: bfloat16 [16, 1408, 2048], P(('dp', 'head'), 'group')
The draws below stay inside these ranges and needn't reach their ends.
Inputs may be any that keep to these rules, and one draw needn't show every extreme that they name: `expert_ids`: each row names 2 different experts; in each aligned block of 128 rows no expert is named by more than 20 rows.
All inputs are finite; a program needn't handle non-finite values.
Results may differ from the reference program's by a relative error of at most 0.012.
Values may be sent and summed in bfloat16 or wider, within the bound.
A program may use at most 128 MiB of HBM per device.

```python
import math
import jax
import jax.numpy as jnp
import numpy as np
from jax import lax

D = 2048
H = 8
HD = 128
FF = 1408
TOP = 2
SEQ = 512
TOKENS = 2048
ROWS_DEV = 128
EXPERTS = 16
CAP = 20
N_DP = 4


def draw_w_qkv(key, part):
    key_base = jax.random.fold_in(key, 11)
    spread = D ** (-0.5)
    values = jax.random.normal(key_base, (3, D, H * HD), jnp.float32) * spread
    return jnp.clip(values, -4.0, 4.0).astype(jnp.bfloat16)


def shard_levels(own_key, shape, split, smallest, high):
    factor_of, own = 1.0, jax.random.fold_in(own_key, 6)
    for dim, blocks in split:
        steps = jnp.exp(jax.random.uniform(jax.random.fold_in(own, dim), (blocks,), jnp.float32, smallest / len(split), high / len(split)))
        factor_of = factor_of * jnp.repeat(steps, shape[dim] // blocks).reshape([-1 if axis == dim else 1 for axis in range(len(shape))])
    return factor_of


def deal_out(own_key, own, number, rows, amount, top, limit, skew):
    order = jax.random.permutation(own_key, amount)
    packed, ordinary = portions_of(amount, rows * top, limit, skew, True), portions_of(amount, rows * top, limit, skew, False)
    places = jnp.arange(amount)

    def named(lengths, offset_by):
        used = int((lengths > 0).sum())
        fixed = max(1, used // 4)
        passed = fixed + (places - fixed + offset_by * (used - fixed)) % max(1, amount - fixed)
        return jnp.zeros((amount,), jnp.int32).at[order[jnp.where(places < fixed, places, passed)]].set(jnp.asarray(lengths, jnp.int32))

    lengths = jnp.where(number % 4 == 0, named(packed, number // 4), named(ordinary, number - number // 4 - 1))
    mixed = jax.random.permutation(jax.random.fold_in(own, 3), amount)
    giver, taker = mixed[0:amount // 2 * 2:2], mixed[1:amount // 2 * 2:2]
    slack = jnp.minimum(lengths[giver] - 1, limit - lengths[taker]) // 2
    slack = jnp.where((giver == order[0]) | (taker == order[0]) | (lengths[taker] == 0), 0, jnp.maximum(slack, 0))
    passed = jax.random.randint(jax.random.fold_in(own, 4), (amount // 2,), 0, 1 << 20) % (slack + 1)
    lengths = lengths.at[giver].add(-passed).at[taker].add(passed)
    items = jnp.searchsorted(jnp.cumsum(lengths), jnp.arange(rows * top), side="right").astype(jnp.int32)
    table = items.reshape(top, rows).T
    table = table[jax.random.permutation(jax.random.fold_in(own, 1), rows)]
    offset_by = jax.random.randint(jax.random.fold_in(own, 2), (rows, 1), 0, top)
    return jnp.take_along_axis(table, (jnp.arange(top)[None, :] + offset_by) % top, axis=1)


def portions_of(amount, total, limit, lean, full):
    weights = [(1 << 20) // math.isqrt(grade ** lean) + 1 for grade in range(1, amount + 1)]
    largest = limit if full else min(limit, max(-(-total // amount), total * weights[0] // sum(weights)))
    least = 1 if total - largest >= amount - 1 else 0
    counts, spare = [largest] + [least] * (amount - 1), total - largest - least * (amount - 1)
    while spare > 0:
        free = [i for i in range(1, amount) if counts[i] < largest] or [i for i in range(1, amount) if counts[i] < limit]
        pool, budget = sum([weights[i] for i in free]), spare
        for i in free:
            addition = min(limit - counts[i], max(1, budget * weights[i] // pool), spare)
            counts[i] = counts[i] + addition
            spare = spare - addition
    return np.array(counts)


def normal_values(stream_key, dims, deviation, most, shards=(), held_as=jnp.bfloat16):
    level = shard_levels(stream_key, dims, shards, -0.22, 0.18) if shards else 1.0
    values = jax.random.normal(stream_key, dims, jnp.float32) * deviation * level
    return jnp.minimum(jnp.maximum(values, -most), most).astype(held_as)


def setup_inputs(seed: int = 0) -> dict:
    keys = jax.random.split(jax.random.key(seed), 11)
    tokens = normal_values(keys[0], (TOKENS, D), 1.0, 6.0, ((0, 16),))
    grad_out = normal_values(keys[1], (TOKENS, D), 1.0, 6.0, ((0, 16),))
    w_qkv = draw_w_qkv(jax.random.fold_in(keys[10], 71), 0)
    w_attn_out = normal_values(keys[3], (H * HD, D), (H * HD) ** -0.5, 0.1875, ((0, 8),))
    gain_attn = jnp.clip(1.0 + 0.15 * jax.random.normal(keys[4], (D,), jnp.float32), 0.25, 1.75)
    gain_ffn = jnp.clip(1.0 + 0.15 * jax.random.normal(keys[5], (D,), jnp.float32), 0.25, 1.75)
    w_gate_up = normal_values(keys[6], (EXPERTS, 2, D, FF), D ** -0.5, 0.125, ((0, 16), (3, 2)))
    w_down = normal_values(keys[7], (EXPERTS, FF, D), FF ** -0.5, 0.15625, ((0, 16), (1, 2)))
    expert_ids_keys = jax.random.split(jax.random.fold_in(keys[8], 1), TOKENS // ROWS_DEV)
    expert_ids_turns = jax.random.permutation(jax.random.fold_in(keys[8], 3), TOKENS // ROWS_DEV)
    expert_ids = jax.vmap(lambda own, number: deal_out(jax.random.fold_in(keys[8], 2), own, number, ROWS_DEV, EXPERTS, TOP, CAP, 2))(expert_ids_keys, expert_ids_turns).reshape((TOKENS, TOP))
    gates = jnp.clip(jnp.exp(math.log(0.5) - 2.3025851 * jax.random.uniform(keys[9], (TOKENS, TOP), jnp.float32) ** shard_levels(keys[9], (TOKENS, TOP), ((0, 16),), -0.2, 0.2)), 0.05, 0.5)
    return {"tokens": tokens, "grad_out": grad_out, "w_qkv": w_qkv, "w_attn_out": w_attn_out, "gain_attn": gain_attn, "gain_ffn": gain_ffn, "w_gate_up": w_gate_up, "w_down": w_down, "expert_ids": expert_ids, "gates": gates}


epsilon = 1e-06

def inverse_rms(values):
    return lax.rsqrt(lax.optimization_barrier(jnp.mean(values * values, axis=-1, keepdims=True)) + epsilon)

def norm_backward(values, scaling, gain, upstream):
    weighted = upstream * gain
    normed = values * scaling
    return scaling * (weighted - normed * lax.optimization_barrier(jnp.mean(weighted * normed, axis=-1, keepdims=True)))

def attention_probs(query_heads, key_heads):
    length = query_heads.shape[0]
    scores = jnp.einsum('qhd,khd->hqk', query_heads.astype(jnp.float32), key_heads.astype(jnp.float32)) * HD ** (-0.5)
    row_pos = lax.broadcasted_iota(jnp.int32, (length, length), 0)
    col_pos = lax.broadcasted_iota(jnp.int32, (length, length), 1)
    scores = jnp.where((col_pos <= row_pos)[None], scores, -1e+30)
    maxima = lax.optimization_barrier(jnp.max(scores, axis=-1, keepdims=True))
    powered = jnp.exp(scores - maxima)
    return powered / lax.optimization_barrier(jnp.sum(powered, axis=-1, keepdims=True))

def attention_forward(bundle):
    query_heads, key_heads, value_heads = bundle
    chances = attention_probs(query_heads, key_heads)
    weights_b = chances.astype(jnp.bfloat16)
    return jnp.einsum('hqk,khd->qhd', weights_b.astype(jnp.float32), value_heads.astype(jnp.float32)).astype(jnp.bfloat16)

def attention_backward(bundle):
    query_heads, key_heads, value_heads, grad_heads = bundle
    chances = attention_probs(query_heads, key_heads)
    weights_b = chances.astype(jnp.bfloat16)
    grad_f = grad_heads.astype(jnp.float32)
    grad_weights = jnp.einsum('qhd,khd->hqk', grad_f, value_heads.astype(jnp.float32))
    grad_values = jnp.einsum('hqk,qhd->khd', weights_b.astype(jnp.float32), grad_f).astype(jnp.bfloat16)
    row_total = lax.optimization_barrier(jnp.sum(chances * grad_weights, axis=-1, keepdims=True))
    grad_scores = (chances * (grad_weights - row_total) * HD ** (-0.5)).astype(jnp.bfloat16)
    grad_queries = jnp.einsum('hqk,khd->qhd', grad_scores.astype(jnp.float32), key_heads.astype(jnp.float32)).astype(jnp.bfloat16)
    grad_keys = jnp.einsum('hqk,qhd->khd', grad_scores.astype(jnp.float32), query_heads.astype(jnp.float32)).astype(jnp.bfloat16)
    return jnp.stack([grad_queries, grad_keys, grad_values])

def reference(tokens, grad_out, w_qkv, w_attn_out, gain_attn, gain_ffn, w_gate_up, w_down, expert_ids, gates):
    tokens_f = tokens.astype(jnp.float32)
    scale_one = inverse_rms(tokens_f)
    normed_one = (tokens_f * scale_one * gain_attn).astype(jnp.bfloat16)
    projected = jnp.stack([jnp.dot(normed_one, w_qkv[which], preferred_element_type=jnp.float32) for which in range(3)]).astype(jnp.bfloat16)
    split_heads = projected.reshape(3, N_DP, SEQ, H, HD)
    mixed = lax.map(attention_forward, (split_heads[0], split_heads[1], split_heads[2]))
    mixed_flat = mixed.reshape(TOKENS, H * HD)
    attn_sum = jnp.dot(mixed_flat, w_attn_out, preferred_element_type=jnp.float32)
    hidden = (tokens_f + attn_sum).astype(jnp.bfloat16)
    hidden_f = hidden.astype(jnp.float32)
    scale_two = inverse_rms(hidden_f)
    normed_two = (hidden_f * scale_two * gain_ffn).astype(jnp.bfloat16)
    grad_f = grad_out.astype(jnp.float32)
    blocks = TOKENS // ROWS_DEV
    flat_ids = expert_ids.reshape(blocks, ROWS_DEV * TOP).astype(jnp.int32)
    onehot = (flat_ids[:, :, None] == jnp.arange(EXPERTS, dtype=jnp.int32)[None, None, :]).astype(jnp.int32)
    earlier = jnp.cumsum(onehot, axis=1) - onehot
    slot_ids = lax.optimization_barrier(jnp.sum(onehot * earlier, axis=2)).astype(jnp.int32)
    token_ids = jnp.broadcast_to(jnp.arange(TOKENS, dtype=jnp.int32).reshape(blocks, ROWS_DEV, 1), (blocks, ROWS_DEV, TOP)).reshape(blocks, ROWS_DEV * TOP)
    block_ids = jnp.broadcast_to(jnp.arange(blocks, dtype=jnp.int32)[:, None], (blocks, ROWS_DEV * TOP))
    table = jnp.full((EXPERTS, blocks, CAP), TOKENS, jnp.int32).at[flat_ids, block_ids, slot_ids].set(token_ids)
    gate_table = jnp.zeros((EXPERTS, blocks, CAP), jnp.float32).at[flat_ids, block_ids, slot_ids].set(gates.reshape(blocks, ROWS_DEV * TOP))
    normed_pad = jnp.concatenate([normed_two, jnp.zeros((1, D), jnp.bfloat16)], axis=0)
    grad_pad = jnp.concatenate([grad_out, jnp.zeros((1, D), jnp.bfloat16)], axis=0)

    def expert_grads(bundle):
        token_index, gate_vals, pair_w, down_w = bundle
        flat_index = token_index.reshape(-1)
        in_rows = normed_pad[flat_index]
        in_grads = (gate_vals.reshape(-1, 1) * grad_pad[flat_index].astype(jnp.float32)).astype(jnp.bfloat16)
        gate_pre = jnp.dot(in_rows, pair_w[0], preferred_element_type=jnp.float32)
        up_pre = jnp.dot(in_rows, pair_w[1], preferred_element_type=jnp.float32)
        sigma = jax.nn.sigmoid(gate_pre)
        active = gate_pre * sigma
        product = (active * up_pre).astype(jnp.bfloat16)
        upstream = jnp.dot(in_grads, down_w.T, preferred_element_type=jnp.float32)
        grad_down_e = jnp.dot(product.T, in_grads, preferred_element_type=jnp.float32).astype(jnp.bfloat16)
        grad_gate = (upstream * up_pre * sigma * (1.0 + gate_pre * (1.0 - sigma))).astype(jnp.bfloat16)
        grad_up = (upstream * active).astype(jnp.bfloat16)
        grad_pair = jnp.stack([jnp.dot(in_rows.T, grad_gate, preferred_element_type=jnp.float32), jnp.dot(in_rows.T, grad_up, preferred_element_type=jnp.float32)]).astype(jnp.bfloat16)
        returned = (jnp.dot(grad_gate, pair_w[0].T, preferred_element_type=jnp.float32) + jnp.dot(grad_up, pair_w[1].T, preferred_element_type=jnp.float32)).astype(jnp.bfloat16)
        return (grad_pair, grad_down_e, returned)
    grad_gate_up, grad_down, returned = lax.map(expert_grads, (table, gate_table, w_gate_up, w_down))
    grad_normed = jnp.zeros((TOKENS + 1, D), jnp.float32).at[table.reshape(-1)].add(returned.reshape(-1, D).astype(jnp.float32))[:TOKENS]
    grad_hidden = grad_f + norm_backward(hidden_f, scale_two, gain_ffn, grad_normed)
    grad_hidden_b = grad_hidden.astype(jnp.bfloat16)
    grad_mixed = jnp.dot(grad_hidden_b, w_attn_out.T, preferred_element_type=jnp.float32).astype(jnp.bfloat16)
    grad_attn_out = jnp.dot(mixed_flat.T, grad_hidden_b, preferred_element_type=jnp.float32)
    grad_heads = grad_mixed.reshape(N_DP, SEQ, H, HD)
    grad_acts = lax.map(attention_backward, (split_heads[0], split_heads[1], split_heads[2], grad_heads))
    grad_acts = jnp.moveaxis(grad_acts, 1, 0).reshape(3, TOKENS, H * HD)
    grad_qkv = jnp.stack([jnp.dot(normed_one.T, grad_acts[which], preferred_element_type=jnp.float32) for which in range(3)])
    grad_normed_one = jnp.dot(grad_acts[0], w_qkv[0].T, preferred_element_type=jnp.float32)
    grad_normed_one = grad_normed_one + jnp.dot(grad_acts[1], w_qkv[1].T, preferred_element_type=jnp.float32)
    grad_normed_one = grad_normed_one + jnp.dot(grad_acts[2], w_qkv[2].T, preferred_element_type=jnp.float32)
    grad_tokens = (grad_hidden + norm_backward(tokens_f, scale_one, gain_attn, grad_normed_one)).astype(jnp.bfloat16)
    return (grad_tokens, grad_qkv, grad_attn_out, grad_gate_up, grad_down)
```

```python
import jax
import jax.numpy as jnp
from jax import lax
from jax.experimental import pallas as pl
from jax.experimental.pallas import tpu as pltpu
from jax.sharding import PartitionSpec as P

HD = 128


MESH = pl.DeviceIdType.MESH
VMEM_LIMIT = 48 * 1024 * 1024

epsilon = 1e-06


def inverse_rms(values):
    return lax.rsqrt(jnp.mean(values * values, axis=-1, keepdims=True) + epsilon)


def norm_backward(values, scaling, gain, upstream):
    weighted = upstream * gain
    normed = values * scaling
    return scaling * (weighted - normed * jnp.mean(weighted * normed, axis=-1, keepdims=True))


def attention_probs(query_heads, key_heads):
    length = query_heads.shape[0]
    scores = jnp.einsum(
        "qhd,khd->hqk", query_heads, key_heads, preferred_element_type=jnp.float32
    ) * HD ** (-0.5)
    row_pos = lax.broadcasted_iota(jnp.int32, (length, length), 0)
    col_pos = lax.broadcasted_iota(jnp.int32, (length, length), 1)
    scores = jnp.where((col_pos <= row_pos)[None], scores, -1e30)
    maxima = jnp.max(scores, axis=-1, keepdims=True)
    powered = jnp.exp(scores - maxima)
    return powered / jnp.sum(powered, axis=-1, keepdims=True)


def expert_work(in_rows, in_grads, w_gate_up, w_down):
    gate_w = w_gate_up[:, 0]
    up_w = w_gate_up[:, 1]
    gate_pre = jnp.einsum("esd,edf->esf", in_rows, gate_w, preferred_element_type=jnp.float32)
    up_pre = jnp.einsum("esd,edf->esf", in_rows, up_w, preferred_element_type=jnp.float32)
    sigma = jax.nn.sigmoid(gate_pre)
    active = gate_pre * sigma
    product = (active * up_pre).astype(jnp.bfloat16)
    upstream = jnp.einsum("esd,efd->esf", in_grads, w_down, preferred_element_type=jnp.float32)
    grad_down = jnp.einsum(
        "esf,esd->efd", product, in_grads, preferred_element_type=jnp.float32
    ).astype(jnp.bfloat16)
    grad_gate = (upstream * up_pre * sigma * (1.0 + gate_pre * (1.0 - sigma))).astype(jnp.bfloat16)
    grad_up = (upstream * active).astype(jnp.bfloat16)
    grad_pair = jnp.stack(
        [
            jnp.einsum("esd,esf->edf", in_rows, grad_gate, preferred_element_type=jnp.float32),
            jnp.einsum("esd,esf->edf", in_rows, grad_up, preferred_element_type=jnp.float32),
        ],
        axis=1,
    ).astype(jnp.bfloat16)
    returned = jnp.einsum("esf,edf->esd", grad_gate, gate_w, preferred_element_type=jnp.float32)
    returned = returned + jnp.einsum(
        "esf,edf->esd", grad_up, up_w, preferred_element_type=jnp.float32
    )
    return (grad_pair, grad_down, returned)


def span(block, size, part=0, length=None):
    length = size if length is None else length
    return pl.ds(pl.multiple_of(block * size + part * length, length), length)


def greet(peers):
    barrier = pltpu.get_barrier_semaphore()
    for peer in peers:
        pl.semaphore_signal(barrier, inc=1, device_id=peer, device_id_type=MESH)
    pl.semaphore_wait(barrier, len(peers))


def remote(src, dst, send_sem, recv_sem, peer):
    return pltpu.make_async_remote_copy(
        src_ref=src, dst_ref=dst, send_sem=send_sem, recv_sem=recv_sem,
        device_id=peer, device_id_type=MESH,
    )


def comm_call(kernel, out, scratch, collective_id, *operands):
    return pl.pallas_call(
        kernel,
        out_shape=out,
        in_specs=[pl.BlockSpec(memory_space=pltpu.VMEM)] * len(operands),
        out_specs=pl.BlockSpec(memory_space=pltpu.VMEM),
        scratch_shapes=scratch,
        compiler_params=pltpu.CompilerParams(
            collective_id=collective_id, has_side_effects=True, vmem_limit_bytes=VMEM_LIMIT
        ),
    )(*operands)


def head_peers(count):
    me = lax.axis_index("head")
    mate = me + 1 - 2 * lax.rem(me, 2)
    return me, mate, [lax.rem(me + 2 * j, count) for j in range(1, count // 2)]


def gather_head(block, collective_id):
    rows, width = block.shape
    count = lax.axis_size("head")
    chunks = 4
    part = rows // chunks
    others = count // 2 - 1

    def kernel(x_ref, o_ref, far_send, far_recv, own_send, own_recv, on_send, on_recv):
        me, mate, far = head_peers(count)
        greet([{"head": mate}] + [{"head": f} for f in far])
        sends, passed = [], []
        for c in range(chunks):
            for j, f in enumerate(far):
                copy = remote(x_ref.at[pl.ds(c * part, part)], o_ref.at[span(me, rows, c, part)],
                              far_send.at[j, c], far_recv.at[j, c], {"head": f})
                copy.start()
                sends.append(copy)
        own = remote(x_ref, o_ref.at[span(me, rows)], own_send, own_recv, {"head": mate})
        own.start()
        o_ref[span(me, rows)] = x_ref[...]
        for c in range(chunks):
            for j in range(others):
                source = lax.rem(me + count - 2 * (j + 1), count)
                place = o_ref.at[span(source, rows, c, part)]
                remote(place, place, far_send.at[j, c], far_recv.at[j, c], {"head": mate}).wait_recv()
                copy = remote(place, place, on_send.at[j, c], on_recv.at[j, c], {"head": mate})
                copy.start()
                passed.append(copy)
        place = o_ref.at[span(mate, rows)]
        remote(place, place, own_send, own_recv, {"head": mate}).wait_recv()
        for c in range(chunks):
            for j in range(others):
                source = lax.rem(mate + count - 2 * (j + 1), count)
                place = o_ref.at[span(source, rows, c, part)]
                remote(place, place, on_send.at[j, c], on_recv.at[j, c], {"head": mate}).wait_recv()
        own.wait_send()
        for copy in sends + passed:
            copy.wait_send()

    dma = pltpu.SemaphoreType.DMA
    many = dma((max(others, 1), chunks))
    return comm_call(
        kernel, jax.ShapeDtypeStruct((count * rows, width), block.dtype),
        [many, many, dma, dma, many, many], collective_id, block,
    )


def sum_to_rows(partial, collective_id):
    count, groups = lax.axis_size("head"), lax.axis_size("group")
    rows, width = partial.shape[0] // count, partial.shape[1]
    chunks = 4
    part = rows // chunks
    pairs = count // 2

    def kernel(p_ref, o_ref, mate_in, far_out, far_in, all_in,
               mate_send, mate_recv, far_send, far_recv, group_send, group_recv):
        me, mate, far = head_peers(count)
        group = lax.axis_index("group")
        rest = [lax.rem(group + k, groups) for k in range(1, groups)]
        greet([{"head": mate}] + [{"head": f} for f in far] + [{"group": g} for g in rest])
        order = list(range(1, pairs)) + [0]
        copies = []
        mates = {}
        for c in range(chunks):
            for j in order:
                block = lax.rem(mate + 2 * j, count)
                copy = remote(p_ref.at[span(block, rows, c, part)],
                              mate_in.at[j, pl.ds(c * part, part)],
                              mate_send.at[j, c], mate_recv.at[j, c], {"head": mate})
                copy.start()
                mates[j, c] = copy
                copies.append(copy)
        fars = {}
        for c in range(chunks):
            at = pl.ds(c * part, part)
            for j in range(1, pairs):
                mates[j, c].wait_recv()
                mine = p_ref[span(far[j - 1], rows, c, part)].astype(jnp.float32)
                far_out[j - 1, at] = (mine + mate_in[j, at].astype(jnp.float32)).astype(jnp.bfloat16)
                copy = remote(far_out.at[j - 1, at], far_in.at[j - 1, at],
                              far_send.at[j - 1, c], far_recv.at[j - 1, c], {"head": far[j - 1]})
                copy.start()
                fars[j, c] = copy
                copies.append(copy)
        crossing = {}
        for c in range(chunks):
            at = pl.ds(c * part, part)
            mates[0, c].wait_recv()
            total = p_ref[span(me, rows, c, part)].astype(jnp.float32)
            total = total + mate_in[0, at].astype(jnp.float32)
            for j in range(1, pairs):
                fars[j, c].wait_recv()
                total = total + far_in[j - 1, at].astype(jnp.float32)
            all_in[group, at] = total.astype(jnp.bfloat16)
            for k, g in enumerate(rest):
                copy = remote(all_in.at[group, at], all_in.at[group, at],
                              group_send.at[k, c], group_recv.at[k, c], {"group": g})
                copy.start()
                crossing[k, c] = copy
                copies.append(copy)
        for c in range(chunks):
            at = pl.ds(c * part, part)
            for k in range(groups - 1):
                source = lax.rem(group + groups - k - 1, groups)
                place = all_in.at[source, at]
                remote(place, place, group_send.at[k, c], group_recv.at[k, c],
                       {"group": rest[k]}).wait_recv()
            total = all_in[0, at].astype(jnp.float32)
            for g in range(1, groups):
                total = total + all_in[g, at].astype(jnp.float32)
            o_ref[at] = total
        for copy in copies:
            copy.wait_send()

    dma = pltpu.SemaphoreType.DMA
    b16 = jnp.bfloat16
    mate_sem, far_sem = dma((pairs, chunks)), dma((max(pairs - 1, 1), chunks))
    group_sem = dma((max(groups - 1, 1), chunks))
    return comm_call(
        kernel, jax.ShapeDtypeStruct((rows, width), jnp.float32),
        [pltpu.VMEM((pairs, rows, width), b16), pltpu.VMEM((max(pairs - 1, 1), rows, width), b16),
         pltpu.VMEM((max(pairs - 1, 1), rows, width), b16), pltpu.VMEM((groups, rows, width), b16),
         mate_sem, mate_sem, far_sem, far_sem, group_sem, group_sem],
        collective_id, partial,
    )


def sum_to_columns(partial, collective_id):
    groups = lax.axis_size("group")
    rows, width = partial.shape
    share = width // groups

    def kernel(p_ref, o_ref, landed, send, recv):
        group = lax.axis_index("group")
        rest = [lax.rem(group + k, groups) for k in range(1, groups)]
        greet([{"group": g} for g in rest])
        copies = []
        for k, g in enumerate(rest):
            copy = remote(p_ref.at[:, span(g, share)], landed.at[k], send.at[k], recv.at[k],
                          {"group": g})
            copy.start()
            copies.append(copy)
        total = p_ref[:, span(group, share)].astype(jnp.float32)
        for k, copy in enumerate(copies):
            copy.wait_recv()
            total = total + landed[k].astype(jnp.float32)
        o_ref[...] = total.astype(jnp.bfloat16)
        for copy in copies:
            copy.wait_send()

    dma = pltpu.SemaphoreType.DMA((max(groups - 1, 1),))
    return comm_call(
        kernel, jax.ShapeDtypeStruct((rows, share), jnp.bfloat16),
        [pltpu.VMEM((max(groups - 1, 1), rows, share), jnp.bfloat16), dma, dma],
        collective_id, partial,
    )


def gather_columns(block, collective_id):
    groups = lax.axis_size("group")
    rows, share = block.shape

    def kernel(x_ref, o_ref, send, recv):
        group = lax.axis_index("group")
        rest = [lax.rem(group + k, groups) for k in range(1, groups)]
        greet([{"group": g} for g in rest])
        copies = []
        for k, g in enumerate(rest):
            copy = remote(x_ref, o_ref.at[:, span(group, share)], send.at[k], recv.at[k],
                          {"group": g})
            copy.start()
            copies.append(copy)
        o_ref[:, span(group, share)] = x_ref[...]
        for k in range(groups - 1):
            source = lax.rem(group + groups - k - 1, groups)
            place = o_ref.at[:, span(source, share)]
            remote(place, place, send.at[k], recv.at[k], {"group": rest[k]}).wait_recv()
        for copy in copies:
            copy.wait_send()

    dma = pltpu.SemaphoreType.DMA((max(groups - 1, 1),))
    return comm_call(
        kernel, jax.ShapeDtypeStruct((rows, groups * share), block.dtype), [dma, dma],
        collective_id, block,
    )


def body(
    tokens, grad_out, w_qkv, w_attn_out, gain_attn, gain_ffn, w_gate_up, w_down, expert_ids, gates
):
    row_count, width = tokens.shape
    seq_len = row_count * lax.axis_size("head")
    head_cols = w_qkv.shape[2]
    head_count = head_cols // HD
    tokens_f = tokens.astype(jnp.float32)
    scale_one = inverse_rms(tokens_f)
    normed_one = (tokens_f * scale_one * gain_attn).astype(jnp.bfloat16)
    shard_rows = gather_head(normed_one, 0)
    fresh = jnp.einsum("rd,idh->irh", shard_rows, w_qkv, preferred_element_type=jnp.float32).astype(
        jnp.bfloat16
    )
    projected = fresh
    gathered = shard_rows
    projected, normed_all = (projected, gathered)
    split_heads = projected.reshape(3, seq_len, head_count, HD)
    query_heads = split_heads[0]
    key_heads = split_heads[1]
    value_heads = split_heads[2]
    chances = attention_probs(query_heads, key_heads)
    weights_b = chances.astype(jnp.bfloat16)
    mixed = (
        jnp.einsum("hqk,khd->qhd", weights_b, value_heads, preferred_element_type=jnp.float32)
        .astype(jnp.bfloat16)
        .reshape(seq_len, head_cols)
    )
    attn_sum = sum_to_rows(
        jnp.dot(mixed, w_attn_out, preferred_element_type=jnp.float32).astype(jnp.bfloat16), 1
    )
    hidden = (tokens_f + attn_sum).astype(jnp.bfloat16)
    hidden_f = hidden.astype(jnp.float32)
    scale_two = inverse_rms(hidden_f)
    normed_two = (hidden_f * scale_two * gain_ffn).astype(jnp.bfloat16)
    grad_f = grad_out.astype(jnp.float32)
    top_count = expert_ids.shape[1]
    owners = lax.axis_size(("dp", "head"))
    local_count = w_gate_up.shape[0]
    expert_count = local_count * owners
    capacity = max(row_count * top_count * 5 // (4 * expert_count), 2)
    flat_ids = expert_ids.reshape(-1)
    onehot = (flat_ids[:, None] == lax.iota(jnp.int32, expert_count)[None, :]).astype(jnp.int32)
    earlier = jnp.cumsum(onehot, axis=0) - onehot
    slot_ids = jnp.sum(onehot * earlier, axis=1)
    targets = flat_ids * capacity + slot_ids
    matches = (lax.iota(jnp.int32, expert_count * capacity)[:, None] == targets[None, :]).reshape(
        expert_count * capacity, row_count, top_count
    )
    picker = jnp.any(matches, axis=2).astype(jnp.bfloat16)
    weigher = jnp.sum(jnp.where(matches, gates[None, :, :], 0.0), axis=2)
    send_rows = (
        jnp.dot(picker, normed_two, preferred_element_type=jnp.float32)
        .astype(jnp.bfloat16)
        .reshape(expert_count, capacity, width)
    )
    send_grads = (
        jnp.dot(
            weigher, grad_f, precision=lax.Precision.HIGHEST, preferred_element_type=jnp.float32
        )
        .astype(jnp.bfloat16)
        .reshape(expert_count, capacity, width)
    )
    got_rows, got_grads = (
        lax.all_to_all(send_rows, ("dp", "head"), split_axis=0, concat_axis=1, tiled=True),
        lax.all_to_all(send_grads, ("dp", "head"), split_axis=0, concat_axis=1, tiled=True),
    )
    grad_pair, grad_down, returned = expert_work(got_rows, got_grads, w_gate_up, w_down)
    shared = sum_to_columns(
        returned.astype(jnp.bfloat16).reshape(expert_count * capacity, width), 2
    ).reshape(local_count, owners * capacity, -1)
    back_half = lax.all_to_all(
        shared, ("dp", "head"), split_axis=1, concat_axis=0, tiled=True
    )
    grad_normed = gather_columns(
        jnp.einsum(
            "cr,cd->rd",
            picker,
            back_half.reshape(expert_count * capacity, -1),
            preferred_element_type=jnp.float32,
        ).astype(jnp.bfloat16),
        3,
    ).astype(jnp.float32)
    grad_hidden = grad_f + norm_backward(hidden_f, scale_two, gain_ffn, grad_normed)
    grad_hidden_b = grad_hidden.astype(jnp.bfloat16)
    shard_rows = gather_head(grad_hidden_b, 4)
    weight_total = jnp.einsum("rh,rd->hd", mixed, shard_rows, preferred_element_type=jnp.float32)
    fresh = jnp.einsum(
        "rd,hd->rh", shard_rows, w_attn_out, preferred_element_type=jnp.float32
    ).astype(jnp.bfloat16)
    grad_mixed = fresh
    grad_out_w, grad_mixed = (weight_total, grad_mixed)
    grad_heads = grad_mixed.reshape(seq_len, head_count, HD)
    grad_weights = jnp.einsum(
        "qhd,khd->hqk", grad_heads, value_heads, preferred_element_type=jnp.float32
    )
    grad_values = jnp.einsum(
        "hqk,qhd->khd", weights_b, grad_heads, preferred_element_type=jnp.float32
    ).astype(jnp.bfloat16)
    row_total = jnp.sum(chances * grad_weights, axis=-1, keepdims=True)
    grad_scores = (chances * (grad_weights - row_total) * HD ** (-0.5)).astype(jnp.bfloat16)
    grad_queries = jnp.einsum(
        "hqk,khd->qhd", grad_scores, key_heads, preferred_element_type=jnp.float32
    ).astype(jnp.bfloat16)
    grad_keys = jnp.einsum(
        "hqk,qhd->khd", grad_scores, query_heads, preferred_element_type=jnp.float32
    ).astype(jnp.bfloat16)
    grad_acts = jnp.stack([grad_queries, grad_keys, grad_values]).reshape(3, seq_len, head_cols)
    grad_proj = jnp.einsum("sd,ish->idh", normed_all, grad_acts, preferred_element_type=jnp.float32)
    grad_normed_one = sum_to_rows(
        jnp.einsum("irh,idh->rd", grad_acts, w_qkv, preferred_element_type=jnp.float32).astype(
            jnp.bfloat16
        ),
        5,
    )
    grad_proj_sum, grad_out_sum = (
        lax.psum_scatter(
            grad_proj.astype(jnp.bfloat16), "dp", scatter_dimension=1, tiled=True
        ).astype(jnp.float32),
        lax.psum_scatter(
            grad_out_w.astype(jnp.bfloat16), "dp", scatter_dimension=1, tiled=True
        ).astype(jnp.float32),
    )
    grad_tokens = (
        grad_hidden + norm_backward(tokens_f, scale_one, gain_attn, grad_normed_one)
    ).astype(jnp.bfloat16)
    return (grad_tokens, grad_proj_sum, grad_out_sum, grad_pair, grad_down)


def solution(mesh):
    return jax.shard_map(
        body,
        mesh=mesh,
        in_specs=(
            P(("dp", "head"), None),
            P(("dp", "head"), None),
            P(None, None, ("head", "group")),
            P(("head", "group"), None),
            P(),
            P(),
            P(("dp", "head"), None, None, "group"),
            P(("dp", "head"), "group", None),
            P(("dp", "head"), None),
            P(("dp", "head"), None),
        ),
        out_specs=(
            P(("dp", "head"), None),
            P(None, "dp", ("head", "group")),
            P(("head", "group"), "dp"),
            P(("dp", "head"), None, None, "group"),
            P(("dp", "head"), "group", None),
        ),
        check_vma=False,
    )
```

```python
import math

import jax
import jax.numpy as jnp
import numpy as np
from jax import lax
from jax.experimental import pallas as pl
from jax.experimental.pallas import tpu as pltpu
from jax.sharding import PartitionSpec as P

HD = 128


MESH = pl.DeviceIdType.MESH
VMEM_LIMIT = 48 * 1024 * 1024

epsilon = 1e-06


def inverse_rms(values):
    return lax.rsqrt(jnp.mean(values * values, axis=-1, keepdims=True) + epsilon)


def norm_backward(values, scaling, gain, upstream):
    weighted = upstream * gain
    normed = values * scaling
    return scaling * (weighted - normed * jnp.mean(weighted * normed, axis=-1, keepdims=True))


def attention_probs(query_heads, key_heads):
    length = query_heads.shape[0]
    scores = jnp.einsum(
        "qhd,khd->hqk", query_heads, key_heads, preferred_element_type=jnp.float32
    ) * HD ** (-0.5)
    row_pos = lax.broadcasted_iota(jnp.int32, (length, length), 0)
    col_pos = lax.broadcasted_iota(jnp.int32, (length, length), 1)
    scores = jnp.where((col_pos <= row_pos)[None], scores, -1e30)
    maxima = jnp.max(scores, axis=-1, keepdims=True)
    powered = jnp.exp(scores - maxima)
    return powered / jnp.sum(powered, axis=-1, keepdims=True)


def expert_work(in_rows, in_grads, w_gate_up, w_down):
    gate_w = w_gate_up[:, 0]
    up_w = w_gate_up[:, 1]
    gate_pre = jnp.einsum("esd,edf->esf", in_rows, gate_w, preferred_element_type=jnp.float32)
    up_pre = jnp.einsum("esd,edf->esf", in_rows, up_w, preferred_element_type=jnp.float32)
    sigma = jax.nn.sigmoid(gate_pre)
    active = gate_pre * sigma
    product = (active * up_pre).astype(jnp.bfloat16)
    upstream = jnp.einsum("esd,efd->esf", in_grads, w_down, preferred_element_type=jnp.float32)
    grad_down = jnp.einsum(
        "esf,esd->efd", product, in_grads, preferred_element_type=jnp.float32
    ).astype(jnp.bfloat16)
    grad_gate = (upstream * up_pre * sigma * (1.0 + gate_pre * (1.0 - sigma))).astype(jnp.bfloat16)
    grad_up = (upstream * active).astype(jnp.bfloat16)
    grad_pair = jnp.stack(
        [
            jnp.einsum("esd,esf->edf", in_rows, grad_gate, preferred_element_type=jnp.float32),
            jnp.einsum("esd,esf->edf", in_rows, grad_up, preferred_element_type=jnp.float32),
        ],
        axis=1,
    ).astype(jnp.bfloat16)
    returned = jnp.einsum("esf,edf->esd", grad_gate, gate_w, preferred_element_type=jnp.float32)
    returned = returned + jnp.einsum(
        "esf,edf->esd", grad_up, up_w, preferred_element_type=jnp.float32
    )
    return (grad_pair, grad_down, returned)


def span(block, size, part=0, length=None):
    length = size if length is None else length
    return pl.ds(pl.multiple_of(block * size + part * length, length), length)


def greet(peers):
    barrier = pltpu.get_barrier_semaphore()
    for peer in peers:
        pl.semaphore_signal(barrier, inc=1, device_id=peer, device_id_type=MESH)
    pl.semaphore_wait(barrier, len(peers))


def remote(src, dst, send_sem, recv_sem, peer):
    return pltpu.make_async_remote_copy(
        src_ref=src, dst_ref=dst, send_sem=send_sem, recv_sem=recv_sem,
        device_id=peer, device_id_type=MESH,
    )


def comm_call(kernel, out, scratch, collective_id, *operands):
    return pl.pallas_call(
        kernel,
        out_shape=out,
        in_specs=[pl.BlockSpec(memory_space=pltpu.VMEM)] * len(operands),
        out_specs=jax.tree.map(lambda _: pl.BlockSpec(memory_space=pltpu.VMEM), out),
        scratch_shapes=scratch,
        compiler_params=pltpu.CompilerParams(
            collective_id=collective_id, has_side_effects=True, vmem_limit_bytes=VMEM_LIMIT
        ),
    )(*operands)


def head_peers(count):
    me = lax.axis_index("head")
    mate = me + 1 - 2 * lax.rem(me, 2)
    return me, mate, [lax.rem(me + 2 * j, count) for j in range(1, count // 2)]


def gather_head(block, collective_id, routed=None):
    rows, width = block.shape
    count = lax.axis_size("head")
    chunks = 4
    part = rows // chunks
    others = count // 2 - 1

    def kernel(*refs):
        if routed is None:
            x_ref, o_ref, far_send, far_recv, own_send, own_recv, on_send, on_recv = refs
        else:
            x_ref, o_ref, far_send, far_recv, own_send, own_recv, on_send, on_recv = (
                refs[0], *refs[routed.inputs + 1 : routed.inputs + 2],
                *refs[routed.inputs + 3 : routed.inputs + 9]
            )
            routed.bind(refs[1 : routed.inputs + 1], refs[routed.inputs + 2], refs[routed.inputs + 9 :])
        me, mate, far = head_peers(count)
        if routed is None:
            greet([{"head": mate}] + [{"head": f} for f in far])
        else:
            routed.greet()
        sends, passed = [], []
        for c in range(chunks):
            for j, f in enumerate(far):
                copy = remote(x_ref.at[pl.ds(c * part, part)], o_ref.at[span(me, rows, c, part)],
                              far_send.at[j, c], far_recv.at[j, c], {"head": f})
                copy.start()
                sends.append(copy)
        own = remote(x_ref, o_ref.at[span(me, rows)], own_send, own_recv, {"head": mate})
        own.start()
        o_ref[span(me, rows)] = x_ref[...]
        if routed is not None:
            routed.start()
        for c in range(chunks):
            for j in range(others):
                source = lax.rem(me + count - 2 * (j + 1), count)
                place = o_ref.at[span(source, rows, c, part)]
                remote(place, place, far_send.at[j, c], far_recv.at[j, c], {"head": mate}).wait_recv()
                copy = remote(place, place, on_send.at[j, c], on_recv.at[j, c], {"head": mate})
                copy.start()
                passed.append(copy)
        place = o_ref.at[span(mate, rows)]
        remote(place, place, own_send, own_recv, {"head": mate}).wait_recv()
        for c in range(chunks):
            for j in range(others):
                source = lax.rem(mate + count - 2 * (j + 1), count)
                place = o_ref.at[span(source, rows, c, part)]
                remote(place, place, on_send.at[j, c], on_recv.at[j, c], {"head": mate}).wait_recv()
        own.wait_send()
        if routed is not None:
            routed.finish()
        for copy in sends + passed:
            copy.wait_send()

    dma = pltpu.SemaphoreType.DMA
    many = dma((max(others, 1), chunks))
    out = jax.ShapeDtypeStruct((count * rows, width), block.dtype)
    scratch = [many, many, dma, dma, many, many]
    if routed is None:
        return comm_call(kernel, out, scratch, collective_id, block)
    return comm_call(
        kernel, (out, routed.out), scratch + routed.scratch, collective_id, block, *routed.operands
    )


def sum_to_rows(partial, collective_id):
    count, groups = lax.axis_size("head"), lax.axis_size("group")
    rows, width = partial.shape[0] // count, partial.shape[1]
    chunks = 4
    part = rows // chunks
    pairs = count // 2

    def kernel(p_ref, o_ref, mate_in, far_out, far_in, all_in,
               mate_send, mate_recv, far_send, far_recv, group_send, group_recv):
        me, mate, far = head_peers(count)
        group = lax.axis_index("group")
        rest = [lax.rem(group + k, groups) for k in range(1, groups)]
        greet([{"head": mate}] + [{"head": f} for f in far] + [{"group": g} for g in rest])
        order = list(range(1, pairs)) + [0]
        copies = []
        mates = {}
        for c in range(chunks):
            for j in order:
                block = lax.rem(mate + 2 * j, count)
                copy = remote(p_ref.at[span(block, rows, c, part)],
                              mate_in.at[j, pl.ds(c * part, part)],
                              mate_send.at[j, c], mate_recv.at[j, c], {"head": mate})
                copy.start()
                mates[j, c] = copy
                copies.append(copy)
        fars = {}
        for c in range(chunks):
            at = pl.ds(c * part, part)
            for j in range(1, pairs):
                mates[j, c].wait_recv()
                mine = p_ref[span(far[j - 1], rows, c, part)].astype(jnp.float32)
                far_out[j - 1, at] = (mine + mate_in[j, at].astype(jnp.float32)).astype(jnp.bfloat16)
                copy = remote(far_out.at[j - 1, at], far_in.at[j - 1, at],
                              far_send.at[j - 1, c], far_recv.at[j - 1, c], {"head": far[j - 1]})
                copy.start()
                fars[j, c] = copy
                copies.append(copy)
        crossing = {}
        for c in range(chunks):
            at = pl.ds(c * part, part)
            mates[0, c].wait_recv()
            total = p_ref[span(me, rows, c, part)].astype(jnp.float32)
            total = total + mate_in[0, at].astype(jnp.float32)
            for j in range(1, pairs):
                fars[j, c].wait_recv()
                total = total + far_in[j - 1, at].astype(jnp.float32)
            all_in[group, at] = total.astype(jnp.bfloat16)
            for k, g in enumerate(rest):
                copy = remote(all_in.at[group, at], all_in.at[group, at],
                              group_send.at[k, c], group_recv.at[k, c], {"group": g})
                copy.start()
                crossing[k, c] = copy
                copies.append(copy)
        for c in range(chunks):
            at = pl.ds(c * part, part)
            for k in range(groups - 1):
                source = lax.rem(group + groups - k - 1, groups)
                place = all_in.at[source, at]
                remote(place, place, group_send.at[k, c], group_recv.at[k, c],
                       {"group": rest[k]}).wait_recv()
            total = all_in[0, at].astype(jnp.float32)
            for g in range(1, groups):
                total = total + all_in[g, at].astype(jnp.float32)
            o_ref[at] = total
        for copy in copies:
            copy.wait_send()

    dma = pltpu.SemaphoreType.DMA
    b16 = jnp.bfloat16
    mate_sem, far_sem = dma((pairs, chunks)), dma((max(pairs - 1, 1), chunks))
    group_sem = dma((max(groups - 1, 1), chunks))
    return comm_call(
        kernel, jax.ShapeDtypeStruct((rows, width), jnp.float32),
        [pltpu.VMEM((pairs, rows, width), b16), pltpu.VMEM((max(pairs - 1, 1), rows, width), b16),
         pltpu.VMEM((max(pairs - 1, 1), rows, width), b16), pltpu.VMEM((groups, rows, width), b16),
         mate_sem, mate_sem, far_sem, far_sem, group_sem, group_sem],
        collective_id, partial,
    )


class Layout:
    def __init__(self, slots, width):
        self.owners = lax.axis_size(("dp", "head"))
        self.groups = lax.axis_size("group")
        self.slots, self.width, self.share = slots, width, width // self.groups
        options = [2**i for i in range(5) if self.share % (128 * 2**i) == 0]
        padded = {c: -(-slots // (16 // c)) * (16 // c) for c in options}
        self.cuts = min(options, key=lambda c: (padded[c], c))
        self.padded = padded[self.cuts]
        self.slab = self.cuts * self.padded
        self.piece = self.share // self.cuts
        self.merged = 16 // math.gcd(slots, 16)
        while self.owners % self.merged:
            self.merged //= 2
        self.blocks = self.owners // self.merged
        self.block_rows = self.merged * slots
        unpack = np.zeros((self.cuts, self.block_rows, self.merged * self.slab), np.float32)
        for c in range(self.cuts):
            for owner in range(self.merged):
                for slot in range(slots):
                    column = owner * self.slab + c * self.padded + slot
                    unpack[c, owner * slots + slot, column] = 1.0
        self.unpack = jnp.asarray(unpack, jnp.bfloat16)
        self.pack = jnp.asarray(unpack.transpose(0, 2, 1), jnp.bfloat16)

    def here(self):
        heads = lax.axis_size("head")
        return lax.axis_index("dp") * heads + lax.axis_index("head")

    def peer(self, owner):
        heads = lax.axis_size("head")
        return {"dp": owner // heads, "head": lax.rem(owner, heads)}

    def greet(self):
        barrier = pltpu.get_barrier_semaphore()
        me, group = self.here(), lax.axis_index("group")

        @pl.loop(1, self.owners)
        def _(k):
            peer = self.peer(lax.rem(me + k, self.owners))
            pl.semaphore_signal(barrier, inc=1, device_id=peer, device_id_type=MESH)

        for k in range(1, self.groups):
            pl.semaphore_signal(
                barrier, inc=1, device_id={"group": lax.rem(group + k, self.groups)},
                device_id_type=MESH,
            )
        pl.semaphore_wait(barrier, self.owners - 1 + self.groups - 1)


class Routed:
    def __init__(self, layout, values, picks, scale=None):
        self.layout = layout
        self.operands = [values, picks, layout.unpack] + ([] if scale is None else [scale])
        self.scaled = scale is not None
        self.inputs = len(self.operands)
        lay = layout
        self.out = jax.ShapeDtypeStruct((lay.owners * lay.slots, lay.width), jnp.bfloat16)
        dma = pltpu.SemaphoreType.DMA
        over, across = dma((lay.owners,)), dma((max(lay.groups - 1, 1), lay.owners))
        self.scratch = [
            pltpu.VMEM((lay.owners * lay.slab, lay.piece), jnp.bfloat16),
            pltpu.VMEM((lay.groups, lay.owners * lay.slab, lay.piece), jnp.bfloat16),
            over, over, across, across,
        ]

    def bind(self, inputs, out, scratch):
        self.values, self.picks, self.unpack = inputs[:3]
        self.scale = inputs[3] if self.scaled else None
        self.got = out
        self.sent, self.landed, self.over_send, self.over_recv, self.across_send, self.across_recv = scratch

    def greet(self):
        self.layout.greet()

    def crossing(self, k, j, source, origin):
        lay, group = self.layout, lax.axis_index("group")
        place = self.landed.at[origin, span(source, lay.slab)]
        return remote(place, place, self.across_send.at[j, k], self.across_recv.at[j, k],
                      {"group": lax.rem(group + j + 1, lay.groups)})

    def start(self):
        lay = self.layout
        me, group = lay.here(), lax.axis_index("group")
        total = jnp.zeros((lay.owners * lay.slab, lay.piece), jnp.float32)
        for c in range(lay.cuts):
            columns = self.values[:, span(group, lay.share, c, lay.piece)]
            total += jnp.dot(self.picks[c], columns, preferred_element_type=jnp.float32)
        if self.scaled:
            total = total * self.scale[...]
        self.sent[...] = total.astype(jnp.bfloat16)

        @pl.loop(1, lay.owners)
        def _(k):
            owner = lax.rem(me + k, lay.owners)
            remote(self.sent.at[span(owner, lay.slab)], self.landed.at[group, span(me, lay.slab)],
                   self.over_send.at[k], self.over_recv.at[k], lay.peer(owner)).start()

        self.landed[group, span(me, lay.slab)] = self.sent[span(me, lay.slab)]
        for j in range(lay.groups - 1):
            self.crossing(0, j, me, group).start()

    def finish(self):
        lay = self.layout
        me, group = lay.here(), lax.axis_index("group")

        @pl.loop(1, lay.owners)
        def _(k):
            source = lax.rem(me + lay.owners - k, lay.owners)
            place = self.landed.at[group, span(source, lay.slab)]
            remote(place, place, self.over_send.at[k], self.over_recv.at[k], lay.peer(source)).wait_recv()
            for j in range(lay.groups - 1):
                self.crossing(k, j, source, group).start()

        @pl.loop(0, lay.owners)
        def _(k):
            source = lax.rem(me + lay.owners - k, lay.owners)
            for j in range(lay.groups - 1):
                origin = lax.rem(group + lay.groups - j - 1, lay.groups)
                self.crossing(k, j, source, origin).wait_recv()

        wide = lay.merged * lay.slab
        for g in range(lay.groups):
            for b in range(lay.blocks):
                block = self.landed[g, b * wide : (b + 1) * wide]
                for c in range(lay.cuts):
                    at = g * lay.share + c * lay.piece
                    self.got[b * lay.block_rows : (b + 1) * lay.block_rows, at : at + lay.piece] = jnp.dot(
                        self.unpack[c], block, preferred_element_type=jnp.float32
                    ).astype(jnp.bfloat16)

        @pl.loop(0, lay.owners)
        def _(k):
            owner = lax.rem(me + k, lay.owners)
            source = lax.rem(me + lay.owners - k, lay.owners)
            for j in range(lay.groups - 1):
                self.crossing(k, j, source, group).wait_send()

            @pl.when(k > 0)
            def _():
                place = self.sent.at[span(owner, lay.slab)]
                remote(place, place, self.over_send.at[k], self.over_recv.at[k],
                       lay.peer(owner)).wait_send()


def route(routed, collective_id):
    def kernel(*refs):
        routed.bind(refs[: routed.inputs], refs[routed.inputs], refs[routed.inputs + 1 :])
        routed.greet()
        routed.start()
        routed.finish()

    return comm_call(kernel, routed.out, routed.scratch, collective_id, *routed.operands)


def route_back(lay, partial, takes, collective_id):
    rows = takes.shape[1]
    others = max(lay.groups - 1, 1)
    wide = lay.merged * lay.slab

    def kernel(p_ref, pack_ref, take_ref, o_ref, landed, sent, back,
               sum_send, sum_recv, over_send, over_recv, across_send, across_recv):
        me, group = lay.here(), lax.axis_index("group")
        rest = [lax.rem(group + k, lay.groups) for k in range(1, lay.groups)]
        first = me // lay.merged
        lay.greet()

        def summing(b, k):
            at = span(lax.rem(first + b + 1, lay.blocks), lay.block_rows)
            return remote(p_ref.at[at, span(rest[k], lay.share)], landed.at[k, at],
                          sum_send.at[k, b], sum_recv.at[k, b], {"group": rest[k]})

        for b in range(lay.blocks):
            for k in range(lay.groups - 1):
                summing(b, k).start()
        for b in range(lay.blocks):
            block = lax.rem(first + b + 1, lay.blocks)
            at = span(block, lay.block_rows)
            total = p_ref[at, span(group, lay.share)].astype(jnp.float32)
            for k in range(lay.groups - 1):
                summing(b, k).wait_recv()
                total = total + landed[k, at].astype(jnp.float32)
            total = total.astype(jnp.bfloat16)
            packed = jnp.zeros((wide, lay.piece), jnp.float32)
            for c in range(lay.cuts):
                packed += jnp.dot(pack_ref[c], total[:, c * lay.piece : (c + 1) * lay.piece],
                                  preferred_element_type=jnp.float32)
            sent[span(block, wide)] = packed.astype(jnp.bfloat16)

            @pl.loop(0, lay.merged)
            def _(j):
                owner = block * lay.merged + j

                @pl.when(owner != me)
                def _():
                    remote(sent.at[span(owner, lay.slab)], back.at[span(me, lay.slab)],
                           over_send.at[owner], over_recv.at[me], lay.peer(owner)).start()

        back[span(me, lay.slab)] = sent[span(me, lay.slab)]

        @pl.loop(1, lay.owners)
        def _(k):
            source = lax.rem(me + k, lay.owners)
            place = back.at[span(source, lay.slab)]
            remote(place, place, over_send.at[source], over_recv.at[source],
                   lay.peer(source)).wait_recv()

        for c in range(lay.cuts):
            o_ref[:, span(group, lay.share, c, lay.piece)] = jnp.dot(
                take_ref[c], back[...], preferred_element_type=jnp.float32
            ).astype(jnp.bfloat16)
        mine = o_ref.at[:, span(group, lay.share)]
        for k in range(lay.groups - 1):
            remote(mine, mine, across_send.at[k], across_recv.at[k], {"group": rest[k]}).start()
        for k in range(lay.groups - 1):
            origin = lax.rem(group + lay.groups - k - 1, lay.groups)
            place = o_ref.at[:, span(origin, lay.share)]
            remote(place, place, across_send.at[k], across_recv.at[k], {"group": rest[k]}).wait_recv()
        for k in range(lay.groups - 1):
            remote(mine, mine, across_send.at[k], across_recv.at[k], {"group": rest[k]}).wait_send()
            for b in range(lay.blocks):
                summing(b, k).wait_send()

        @pl.loop(1, lay.owners)
        def _(k):
            owner = lax.rem(me + k, lay.owners)
            place = sent.at[span(owner, lay.slab)]
            remote(place, place, over_send.at[owner], over_recv.at[owner], lay.peer(owner)).wait_send()

    dma = pltpu.SemaphoreType.DMA
    b16 = jnp.bfloat16
    return comm_call(
        kernel, jax.ShapeDtypeStruct((rows, lay.width), b16),
        [pltpu.VMEM((others, lay.owners * lay.slots, lay.share), b16),
         pltpu.VMEM((lay.owners * lay.slab, lay.piece), b16),
         pltpu.VMEM((lay.owners * lay.slab, lay.piece), b16),
         dma((others, lay.blocks)), dma((others, lay.blocks)),
         dma((lay.owners,)), dma((lay.owners,)), dma((others,)), dma((others,))],
        collective_id, partial, lay.pack, takes,
    )


def body(
    tokens, grad_out, w_qkv, w_attn_out, gain_attn, gain_ffn, w_gate_up, w_down, expert_ids, gates
):
    row_count, width = tokens.shape
    seq_len = row_count * lax.axis_size("head")
    head_cols = w_qkv.shape[2]
    head_count = head_cols // HD
    tokens_f = tokens.astype(jnp.float32)
    scale_one = inverse_rms(tokens_f)
    normed_one = (tokens_f * scale_one * gain_attn).astype(jnp.bfloat16)
    top_count = expert_ids.shape[1]
    owners = lax.axis_size(("dp", "head"))
    local_count = w_gate_up.shape[0]
    expert_count = local_count * owners
    capacity = max(row_count * top_count * 5 // (4 * expert_count), 2)
    flat_ids = expert_ids.reshape(-1)
    onehot = (flat_ids[:, None] == lax.iota(jnp.int32, expert_count)[None, :]).astype(jnp.int32)
    earlier = jnp.cumsum(onehot, axis=0) - onehot
    slot_ids = jnp.sum(onehot * earlier, axis=1)
    slots = local_count * capacity
    lay = Layout(slots, width)
    owner_ids = flat_ids // local_count
    places = owner_ids * lay.slab + (flat_ids % local_count) * capacity + slot_ids
    slab_rows = owners * lay.slab
    row_ids = lax.iota(jnp.int32, slab_rows)
    cut_ids = row_ids % lay.slab // lay.padded
    plain_ids = row_ids - cut_ids * lay.padded
    places = places.reshape(row_count, top_count)
    matches = plain_ids[:, None, None] == places[None]
    row_gates = jnp.sum(jnp.where(matches, gates[None], 0.0), axis=(1, 2))[:, None]
    cuts = lax.iota(jnp.int32, lay.cuts)
    picks = (
        jnp.any(matches, axis=2)[None] & (cut_ids[None, :] == cuts[:, None])[:, :, None]
    ).astype(jnp.bfloat16)
    takes = (
        jnp.any(places[:, :, None] == plain_ids[None, None, :], axis=1)[None]
        & (cut_ids[None, :] == cuts[:, None])[:, None, :]
    ).astype(jnp.bfloat16)
    shard_rows, got_grads = gather_head(normed_one, 0, Routed(lay, grad_out, picks, row_gates))
    fresh = jnp.einsum("rd,idh->irh", shard_rows, w_qkv, preferred_element_type=jnp.float32).astype(
        jnp.bfloat16
    )
    projected = fresh
    gathered = shard_rows
    projected, normed_all = (projected, gathered)
    split_heads = projected.reshape(3, seq_len, head_count, HD)
    query_heads = split_heads[0]
    key_heads = split_heads[1]
    value_heads = split_heads[2]
    chances = attention_probs(query_heads, key_heads)
    weights_b = chances.astype(jnp.bfloat16)
    mixed = (
        jnp.einsum("hqk,khd->qhd", weights_b, value_heads, preferred_element_type=jnp.float32)
        .astype(jnp.bfloat16)
        .reshape(seq_len, head_cols)
    )
    attn_sum = sum_to_rows(
        jnp.dot(mixed, w_attn_out, preferred_element_type=jnp.float32).astype(jnp.bfloat16), 1
    )
    hidden = (tokens_f + attn_sum).astype(jnp.bfloat16)
    hidden_f = hidden.astype(jnp.float32)
    scale_two = inverse_rms(hidden_f)
    normed_two = (hidden_f * scale_two * gain_ffn).astype(jnp.bfloat16)
    grad_f = grad_out.astype(jnp.float32)
    got_rows = route(Routed(lay, normed_two, picks), 2)

    def by_expert(got):
        got = got.reshape(owners, local_count, capacity, width)
        return jnp.swapaxes(got, 0, 1).reshape(local_count, owners * capacity, width)

    got_rows, got_grads = by_expert(got_rows), by_expert(got_grads)
    grad_pair, grad_down, returned = expert_work(got_rows, got_grads, w_gate_up, w_down)
    returned = returned.astype(jnp.bfloat16).reshape(local_count, owners, capacity, width)
    returned = jnp.swapaxes(returned, 0, 1).reshape(owners * slots, width)
    grad_normed = route_back(lay, returned, takes, 3).astype(jnp.float32)
    grad_hidden = grad_f + norm_backward(hidden_f, scale_two, gain_ffn, grad_normed)
    grad_hidden_b = grad_hidden.astype(jnp.bfloat16)
    shard_rows = gather_head(grad_hidden_b, 4)
    weight_total = jnp.einsum("rh,rd->hd", mixed, shard_rows, preferred_element_type=jnp.float32)
    fresh = jnp.einsum(
        "rd,hd->rh", shard_rows, w_attn_out, preferred_element_type=jnp.float32
    ).astype(jnp.bfloat16)
    grad_mixed = fresh
    grad_out_w, grad_mixed = (weight_total, grad_mixed)
    grad_heads = grad_mixed.reshape(seq_len, head_count, HD)
    grad_weights = jnp.einsum(
        "qhd,khd->hqk", grad_heads, value_heads, preferred_element_type=jnp.float32
    )
    grad_values = jnp.einsum(
        "hqk,qhd->khd", weights_b, grad_heads, preferred_element_type=jnp.float32
    ).astype(jnp.bfloat16)
    row_total = jnp.sum(chances * grad_weights, axis=-1, keepdims=True)
    grad_scores = (chances * (grad_weights - row_total) * HD ** (-0.5)).astype(jnp.bfloat16)
    grad_queries = jnp.einsum(
        "hqk,khd->qhd", grad_scores, key_heads, preferred_element_type=jnp.float32
    ).astype(jnp.bfloat16)
    grad_keys = jnp.einsum(
        "hqk,qhd->khd", grad_scores, query_heads, preferred_element_type=jnp.float32
    ).astype(jnp.bfloat16)
    grad_acts = jnp.stack([grad_queries, grad_keys, grad_values]).reshape(3, seq_len, head_cols)
    grad_proj = jnp.einsum("sd,ish->idh", normed_all, grad_acts, preferred_element_type=jnp.float32)
    grad_normed_one = sum_to_rows(
        jnp.einsum("irh,idh->rd", grad_acts, w_qkv, preferred_element_type=jnp.float32).astype(
            jnp.bfloat16
        ),
        5,
    )
    grad_proj_sum, grad_out_sum = (
        lax.psum_scatter(
            grad_proj.astype(jnp.bfloat16), "dp", scatter_dimension=1, tiled=True
        ).astype(jnp.float32),
        lax.psum_scatter(
            grad_out_w.astype(jnp.bfloat16), "dp", scatter_dimension=1, tiled=True
        ).astype(jnp.float32),
    )
    grad_tokens = (
        grad_hidden + norm_backward(tokens_f, scale_one, gain_attn, grad_normed_one)
    ).astype(jnp.bfloat16)
    return (grad_tokens, grad_proj_sum, grad_out_sum, grad_pair, grad_down)


def solution(mesh):
    return jax.shard_map(
        body,
        mesh=mesh,
        in_specs=(
            P(("dp", "head"), None),
            P(("dp", "head"), None),
            P(None, None, ("head", "group")),
            P(("head", "group"), None),
            P(),
            P(),
            P(("dp", "head"), None, None, "group"),
            P(("dp", "head"), "group", None),
            P(("dp", "head"), None),
            P(("dp", "head"), None),
        ),
        out_specs=(
            P(("dp", "head"), None),
            P(None, "dp", ("head", "group")),
            P(("head", "group"), "dp"),
            P(("dp", "head"), None, None, "group"),
            P(("dp", "head"), "group", None),
        ),
        check_vma=False,
    )
```

```python
import math

import jax
import jax.numpy as jnp
import numpy as np
from jax import lax
from jax.experimental import pallas as pl
from jax.experimental.pallas import tpu as pltpu
from jax.sharding import PartitionSpec as P

HD = 128


MESH = pl.DeviceIdType.MESH
VMEM_LIMIT = 48 * 1024 * 1024

epsilon = 1e-06


def inverse_rms(values):
    return lax.rsqrt(jnp.mean(values * values, axis=-1, keepdims=True) + epsilon)


def norm_backward(values, scaling, gain, upstream):
    weighted = upstream * gain
    normed = values * scaling
    return scaling * (weighted - normed * jnp.mean(weighted * normed, axis=-1, keepdims=True))


def attention_probs(query_heads, key_heads):
    length = query_heads.shape[0]
    scores = jnp.einsum(
        "qhd,khd->hqk", query_heads, key_heads, preferred_element_type=jnp.float32
    ) * HD ** (-0.5)
    row_pos = lax.broadcasted_iota(jnp.int32, (length, length), 0)
    col_pos = lax.broadcasted_iota(jnp.int32, (length, length), 1)
    scores = jnp.where((col_pos <= row_pos)[None], scores, -1e30)
    maxima = jnp.max(scores, axis=-1, keepdims=True)
    powered = jnp.exp(scores - maxima)
    return powered / jnp.sum(powered, axis=-1, keepdims=True)


def expert_work(in_rows, in_grads, w_gate_up, w_down):
    gate_w = w_gate_up[:, 0]
    up_w = w_gate_up[:, 1]
    gate_pre = jnp.einsum("esd,edf->esf", in_rows, gate_w, preferred_element_type=jnp.float32)
    up_pre = jnp.einsum("esd,edf->esf", in_rows, up_w, preferred_element_type=jnp.float32)
    sigma = jax.nn.sigmoid(gate_pre)
    active = gate_pre * sigma
    product = (active * up_pre).astype(jnp.bfloat16)
    upstream = jnp.einsum("esd,efd->esf", in_grads, w_down, preferred_element_type=jnp.float32)
    grad_down = jnp.einsum(
        "esf,esd->efd", product, in_grads, preferred_element_type=jnp.float32
    ).astype(jnp.bfloat16)
    grad_gate = (upstream * up_pre * sigma * (1.0 + gate_pre * (1.0 - sigma))).astype(jnp.bfloat16)
    grad_up = (upstream * active).astype(jnp.bfloat16)
    grad_pair = jnp.stack(
        [
            jnp.einsum("esd,esf->edf", in_rows, grad_gate, preferred_element_type=jnp.float32),
            jnp.einsum("esd,esf->edf", in_rows, grad_up, preferred_element_type=jnp.float32),
        ],
        axis=1,
    ).astype(jnp.bfloat16)
    returned = jnp.einsum("esf,edf->esd", grad_gate, gate_w, preferred_element_type=jnp.float32)
    returned = returned + jnp.einsum(
        "esf,edf->esd", grad_up, up_w, preferred_element_type=jnp.float32
    )
    return (grad_pair, grad_down, returned)


def span(block, size, part=0, length=None):
    length = size if length is None else length
    return pl.ds(pl.multiple_of(block * size + part * length, length), length)


def greet(peers):
    barrier = pltpu.get_barrier_semaphore()
    for peer in peers:
        pl.semaphore_signal(barrier, inc=1, device_id=peer, device_id_type=MESH)
    pl.semaphore_wait(barrier, len(peers))


def remote(src, dst, send_sem, recv_sem, peer):
    return pltpu.make_async_remote_copy(
        src_ref=src, dst_ref=dst, send_sem=send_sem, recv_sem=recv_sem,
        device_id=peer, device_id_type=MESH,
    )


def comm_call(kernel, out, scratch, collective_id, *operands):
    return pl.pallas_call(
        kernel,
        out_shape=out,
        in_specs=[pl.BlockSpec(memory_space=pltpu.VMEM)] * len(operands),
        out_specs=jax.tree.map(lambda _: pl.BlockSpec(memory_space=pltpu.VMEM), out),
        scratch_shapes=scratch,
        compiler_params=pltpu.CompilerParams(
            collective_id=collective_id, has_side_effects=True, vmem_limit_bytes=VMEM_LIMIT
        ),
    )(*operands)


def head_peers(count):
    me = lax.axis_index("head")
    mate = me + 1 - 2 * lax.rem(me, 2)
    return me, mate, [lax.rem(me + 2 * j, count) for j in range(1, count // 2)]


def gather_head(block, collective_id, routed=None):
    rows, width = block.shape
    count = lax.axis_size("head")
    chunks = 4
    part = rows // chunks
    others = count // 2 - 1

    def kernel(*refs):
        if routed is None:
            x_ref, o_ref, far_send, far_recv, own_send, own_recv, on_send, on_recv = refs
        else:
            x_ref, o_ref, far_send, far_recv, own_send, own_recv, on_send, on_recv = (
                refs[0], *refs[routed.inputs + 1 : routed.inputs + 2],
                *refs[routed.inputs + 3 : routed.inputs + 9]
            )
            routed.bind(refs[1 : routed.inputs + 1], refs[routed.inputs + 2], refs[routed.inputs + 9 :])
        me, mate, far = head_peers(count)
        if routed is None:
            greet([{"head": mate}] + [{"head": f} for f in far])
        else:
            routed.greet()
        sends, passed = [], []
        if routed is not None:
            routed.start()
        for c in range(chunks):
            for j, f in enumerate(far):
                copy = remote(x_ref.at[pl.ds(c * part, part)], o_ref.at[span(me, rows, c, part)],
                              far_send.at[j, c], far_recv.at[j, c], {"head": f})
                copy.start()
                sends.append(copy)
        own = remote(x_ref, o_ref.at[span(me, rows)], own_send, own_recv, {"head": mate})
        own.start()
        o_ref[span(me, rows)] = x_ref[...]
        for c in range(chunks):
            if routed is not None:
                routed.forward(c, chunks)
            for j in range(others):
                source = lax.rem(me + count - 2 * (j + 1), count)
                place = o_ref.at[span(source, rows, c, part)]
                remote(place, place, far_send.at[j, c], far_recv.at[j, c], {"head": mate}).wait_recv()
                copy = remote(place, place, on_send.at[j, c], on_recv.at[j, c], {"head": mate})
                copy.start()
                passed.append(copy)
        place = o_ref.at[span(mate, rows)]
        remote(place, place, own_send, own_recv, {"head": mate}).wait_recv()
        for c in range(chunks):
            for j in range(others):
                source = lax.rem(mate + count - 2 * (j + 1), count)
                place = o_ref.at[span(source, rows, c, part)]
                remote(place, place, on_send.at[j, c], on_recv.at[j, c], {"head": mate}).wait_recv()
        own.wait_send()
        if routed is not None:
            routed.finish()
        for copy in sends + passed:
            copy.wait_send()

    dma = pltpu.SemaphoreType.DMA
    many = dma((max(others, 1), chunks))
    out = jax.ShapeDtypeStruct((count * rows, width), block.dtype)
    scratch = [many, many, dma, dma, many, many]
    if routed is None:
        return comm_call(kernel, out, scratch, collective_id, block)
    return comm_call(
        kernel, (out, routed.out), scratch + routed.scratch, collective_id, block, *routed.operands
    )


def gather_head_split(block, collective_id):
    rows, width = block.shape
    count, groups = lax.axis_size("head"), lax.axis_size("group")
    part = 16
    chunks = rows // (part * groups)
    share = part * chunks
    others = count // 2 - 1

    def kernel(x_ref, o_ref, far_send, far_recv, own_send, own_recv,
               across_send, across_recv, on_send, on_recv):
        me, mate, far = head_peers(count)
        group = lax.axis_index("group")
        rest = [lax.rem(group + k, groups) for k in range(1, groups)]
        greet([{"head": mate}] + [{"head": f} for f in far] + [{"group": g} for g in rest])
        copies = []

        def place(block, owner_group, c):
            start = pl.multiple_of(block * rows + owner_group * share + c * part, part)
            return o_ref.at[pl.ds(start, part)]

        for c in range(chunks):
            for j, f in enumerate(far):
                copy = remote(x_ref.at[span(group, share, c, part)], place(me, group, c),
                              far_send.at[j, c], far_recv.at[j, c], {"head": f})
                copy.start()
                copies.append(copy)
        own = remote(x_ref, o_ref.at[span(me, rows)], own_send, own_recv, {"head": mate})
        own.start()
        o_ref[span(me, rows)] = x_ref[...]

        def pass_on(j, k, c, at):
            copy = remote(at, at, on_send.at[j, k, c], on_recv.at[j, k, c], {"head": mate})
            copy.start()
            copies.append(copy)

        for c in range(chunks):
            for j in range(others):
                at = place(lax.rem(me + count - 2 * (j + 1), count), group, c)
                remote(at, at, far_send.at[j, c], far_recv.at[j, c], {"head": mate}).wait_recv()
                for k, g in enumerate(rest):
                    copy = remote(at, at, across_send.at[j, k, c], across_recv.at[j, k, c], {"group": g})
                    copy.start()
                    copies.append(copy)
                pass_on(j, 0, c, at)
        origins = [lax.rem(group + groups - k - 1, groups) for k in range(groups - 1)]
        for c in range(chunks):
            for j in range(others):
                for k, origin in enumerate(origins):
                    at = place(lax.rem(me + count - 2 * (j + 1), count), origin, c)
                    remote(at, at, across_send.at[j, k, c], across_recv.at[j, k, c],
                           {"group": rest[k]}).wait_recv()
                    pass_on(j, k + 1, c, at)
        at = o_ref.at[span(mate, rows)]
        remote(at, at, own_send, own_recv, {"head": mate}).wait_recv()
        for c in range(chunks):
            for j in range(others):
                for k, origin in enumerate([group] + origins):
                    at = place(lax.rem(mate + count - 2 * (j + 1), count), origin, c)
                    remote(at, at, on_send.at[j, k, c], on_recv.at[j, k, c],
                           {"head": mate}).wait_recv()
        own.wait_send()
        for copy in copies:
            copy.wait_send()

    dma = pltpu.SemaphoreType.DMA
    far_sem = dma((max(others, 1), chunks))
    across = dma((max(others, 1), max(groups - 1, 1), chunks))
    on = dma((max(others, 1), groups, chunks))
    return comm_call(
        kernel, jax.ShapeDtypeStruct((count * rows, width), block.dtype),
        [far_sem, far_sem, dma, dma, across, across, on, on], collective_id, block,
    )


def sum_to_rows(partial, collective_id):
    count, groups = lax.axis_size("head"), lax.axis_size("group")
    rows, width = partial.shape[0] // count, partial.shape[1]
    chunks = 8
    part = rows // chunks
    pairs = count // 2

    def kernel(p_ref, o_ref, mate_in, far_out, far_in, all_in,
               mate_send, mate_recv, far_send, far_recv, group_send, group_recv):
        me, mate, far = head_peers(count)
        group = lax.axis_index("group")
        rest = [lax.rem(group + k, groups) for k in range(1, groups)]
        greet([{"head": mate}] + [{"head": f} for f in far] + [{"group": g} for g in rest])
        order = list(range(1, pairs)) + [0]
        copies = []
        mates = {}
        for c in range(chunks):
            for j in order:
                block = lax.rem(mate + 2 * j, count)
                copy = remote(p_ref.at[span(block, rows, c, part)],
                              mate_in.at[j, pl.ds(c * part, part)],
                              mate_send.at[j, c], mate_recv.at[j, c], {"head": mate})
                copy.start()
                mates[j, c] = copy
                copies.append(copy)
        fars = {}
        for c in range(chunks):
            at = pl.ds(c * part, part)
            for j in range(1, pairs):
                mates[j, c].wait_recv()
                mine = p_ref[span(far[j - 1], rows, c, part)].astype(jnp.float32)
                far_out[j - 1, at] = (mine + mate_in[j, at].astype(jnp.float32)).astype(jnp.bfloat16)
                copy = remote(far_out.at[j - 1, at], far_in.at[j - 1, at],
                              far_send.at[j - 1, c], far_recv.at[j - 1, c], {"head": far[j - 1]})
                copy.start()
                fars[j, c] = copy
                copies.append(copy)
        crossing = {}
        for c in range(chunks):
            at = pl.ds(c * part, part)
            mates[0, c].wait_recv()
            total = p_ref[span(me, rows, c, part)].astype(jnp.float32)
            total = total + mate_in[0, at].astype(jnp.float32)
            for j in range(1, pairs):
                fars[j, c].wait_recv()
                total = total + far_in[j - 1, at].astype(jnp.float32)
            all_in[group, at] = total.astype(jnp.bfloat16)
            for k, g in enumerate(rest):
                copy = remote(all_in.at[group, at], all_in.at[group, at],
                              group_send.at[k, c], group_recv.at[k, c], {"group": g})
                copy.start()
                crossing[k, c] = copy
                copies.append(copy)
        for c in range(chunks):
            at = pl.ds(c * part, part)
            for k in range(groups - 1):
                source = lax.rem(group + groups - k - 1, groups)
                place = all_in.at[source, at]
                remote(place, place, group_send.at[k, c], group_recv.at[k, c],
                       {"group": rest[k]}).wait_recv()
            total = all_in[0, at].astype(jnp.float32)
            for g in range(1, groups):
                total = total + all_in[g, at].astype(jnp.float32)
            o_ref[at] = total
        for copy in copies:
            copy.wait_send()

    dma = pltpu.SemaphoreType.DMA
    b16 = jnp.bfloat16
    mate_sem, far_sem = dma((pairs, chunks)), dma((max(pairs - 1, 1), chunks))
    group_sem = dma((max(groups - 1, 1), chunks))
    return comm_call(
        kernel, jax.ShapeDtypeStruct((rows, width), jnp.float32),
        [pltpu.VMEM((pairs, rows, width), b16), pltpu.VMEM((max(pairs - 1, 1), rows, width), b16),
         pltpu.VMEM((max(pairs - 1, 1), rows, width), b16), pltpu.VMEM((groups, rows, width), b16),
         mate_sem, mate_sem, far_sem, far_sem, group_sem, group_sem],
        collective_id, partial,
    )


class Layout:
    def __init__(self, slots, width):
        self.owners = lax.axis_size(("dp", "head"))
        self.groups = lax.axis_size("group")
        self.slots, self.width, self.share = slots, width, width // self.groups
        options = [2**i for i in range(5) if self.share % (128 * 2**i) == 0]
        padded = {c: -(-slots // (16 // c)) * (16 // c) for c in options}
        self.cuts = min(options, key=lambda c: (padded[c], c))
        self.padded = padded[self.cuts]
        self.slab = self.cuts * self.padded
        self.piece = self.share // self.cuts
        self.merged = 16 // math.gcd(slots, 16)
        while self.owners % self.merged:
            self.merged //= 2
        self.blocks = self.owners // self.merged
        self.block_rows = self.merged * slots
        unpack = np.zeros((self.cuts, self.block_rows, self.merged * self.slab), np.float32)
        for c in range(self.cuts):
            for owner in range(self.merged):
                for slot in range(slots):
                    column = owner * self.slab + c * self.padded + slot
                    unpack[c, owner * slots + slot, column] = 1.0
        self.unpack = jnp.asarray(unpack, jnp.bfloat16)
        self.pack = jnp.asarray(unpack.transpose(0, 2, 1), jnp.bfloat16)

    def here(self):
        heads = lax.axis_size("head")
        return lax.axis_index("dp") * heads + lax.axis_index("head")

    def peer(self, owner):
        heads = lax.axis_size("head")
        return {"dp": owner // heads, "head": lax.rem(owner, heads)}

    def greet(self):
        barrier = pltpu.get_barrier_semaphore()
        me, group = self.here(), lax.axis_index("group")

        @pl.loop(1, self.owners)
        def _(k):
            peer = self.peer(lax.rem(me + k, self.owners))
            pl.semaphore_signal(barrier, inc=1, device_id=peer, device_id_type=MESH)

        for k in range(1, self.groups):
            pl.semaphore_signal(
                barrier, inc=1, device_id={"group": lax.rem(group + k, self.groups)},
                device_id_type=MESH,
            )
        pl.semaphore_wait(barrier, self.owners - 1 + self.groups - 1)


class Routed:
    def __init__(self, layout, values, picks, scale=None):
        self.layout = layout
        self.operands = [values, picks, layout.unpack] + ([] if scale is None else [scale])
        self.scaled = scale is not None
        self.inputs = len(self.operands)
        lay = layout
        self.out = jax.ShapeDtypeStruct((lay.owners * lay.slots, lay.width), jnp.bfloat16)
        dma = pltpu.SemaphoreType.DMA
        over, across = dma((lay.owners,)), dma((max(lay.groups - 1, 1), lay.owners))
        self.scratch = [
            pltpu.VMEM((lay.owners * lay.slab, lay.piece), jnp.bfloat16),
            pltpu.VMEM((lay.groups, lay.owners * lay.slab, lay.piece), jnp.bfloat16),
            over, over, across, across,
        ]

    def bind(self, inputs, out, scratch):
        self.values, self.picks, self.unpack = inputs[:3]
        self.scale = inputs[3] if self.scaled else None
        self.got = out
        self.sent, self.landed, self.over_send, self.over_recv, self.across_send, self.across_recv = scratch

    def greet(self):
        self.layout.greet()

    def crossing(self, k, j, source, origin):
        lay, group = self.layout, lax.axis_index("group")
        place = self.landed.at[origin, span(source, lay.slab)]
        return remote(place, place, self.across_send.at[j, k], self.across_recv.at[j, k],
                      {"group": lax.rem(group + j + 1, lay.groups)})

    def start(self):
        lay = self.layout
        me, group = lay.here(), lax.axis_index("group")
        total = jnp.zeros((lay.owners * lay.slab, lay.piece), jnp.float32)
        for c in range(lay.cuts):
            columns = self.values[:, span(group, lay.share, c, lay.piece)]
            total += jnp.dot(self.picks[c], columns, preferred_element_type=jnp.float32)
        if self.scaled:
            total = total * self.scale[...]
        self.sent[...] = total.astype(jnp.bfloat16)

        @pl.loop(1, lay.owners)
        def _(k):
            owner = lax.rem(me + k, lay.owners)
            remote(self.sent.at[span(owner, lay.slab)], self.landed.at[group, span(me, lay.slab)],
                   self.over_send.at[k], self.over_recv.at[k], lay.peer(owner)).start()

        self.landed[group, span(me, lay.slab)] = self.sent[span(me, lay.slab)]
        for j in range(lay.groups - 1):
            self.crossing(0, j, me, group).start()

    def forward(self, part=0, parts=1):
        lay = self.layout
        me, group = lay.here(), lax.axis_index("group")
        begin = 1 + part * (lay.owners - 1) // parts
        end = 1 + (part + 1) * (lay.owners - 1) // parts

        @pl.loop(begin, end)
        def _(k):
            source = lax.rem(me + lay.owners - k, lay.owners)
            place = self.landed.at[group, span(source, lay.slab)]
            remote(place, place, self.over_send.at[k], self.over_recv.at[k], lay.peer(source)).wait_recv()
            for j in range(lay.groups - 1):
                self.crossing(k, j, source, group).start()

    def finish(self):
        lay = self.layout
        me, group = lay.here(), lax.axis_index("group")

        @pl.loop(0, lay.owners)
        def _(k):
            source = lax.rem(me + lay.owners - k, lay.owners)
            for j in range(lay.groups - 1):
                origin = lax.rem(group + lay.groups - j - 1, lay.groups)
                self.crossing(k, j, source, origin).wait_recv()

        wide = lay.merged * lay.slab
        for g in range(lay.groups):
            for b in range(lay.blocks):
                block = self.landed[g, b * wide : (b + 1) * wide]
                for c in range(lay.cuts):
                    at = g * lay.share + c * lay.piece
                    self.got[b * lay.block_rows : (b + 1) * lay.block_rows, at : at + lay.piece] = jnp.dot(
                        self.unpack[c], block, preferred_element_type=jnp.float32
                    ).astype(jnp.bfloat16)

        @pl.loop(0, lay.owners)
        def _(k):
            owner = lax.rem(me + k, lay.owners)
            source = lax.rem(me + lay.owners - k, lay.owners)
            for j in range(lay.groups - 1):
                self.crossing(k, j, source, group).wait_send()

            @pl.when(k > 0)
            def _():
                place = self.sent.at[span(owner, lay.slab)]
                remote(place, place, self.over_send.at[k], self.over_recv.at[k],
                       lay.peer(owner)).wait_send()


def route(routed, collective_id):
    def kernel(*refs):
        routed.bind(refs[: routed.inputs], refs[routed.inputs], refs[routed.inputs + 1 :])
        routed.greet()
        routed.start()
        routed.forward()
        routed.finish()

    return comm_call(kernel, routed.out, routed.scratch, collective_id, *routed.operands)


def route_back(lay, partial, takes, collective_id):
    rows = takes.shape[1]
    others = max(lay.groups - 1, 1)
    wide = lay.merged * lay.slab

    def kernel(p_ref, pack_ref, take_ref, o_ref, landed, sent, back,
               sum_send, sum_recv, over_send, over_recv, across_send, across_recv):
        me, group = lay.here(), lax.axis_index("group")
        rest = [lax.rem(group + k, lay.groups) for k in range(1, lay.groups)]
        first = me // lay.merged
        lay.greet()

        def summing(b, k):
            at = span(lax.rem(first + b + 1, lay.blocks), lay.block_rows)
            return remote(p_ref.at[at, span(rest[k], lay.share)], landed.at[k, at],
                          sum_send.at[k, b], sum_recv.at[k, b], {"group": rest[k]})

        for b in range(lay.blocks):
            for k in range(lay.groups - 1):
                summing(b, k).start()
        for b in range(lay.blocks):
            block = lax.rem(first + b + 1, lay.blocks)
            at = span(block, lay.block_rows)
            total = p_ref[at, span(group, lay.share)].astype(jnp.float32)
            for k in range(lay.groups - 1):
                summing(b, k).wait_recv()
                total = total + landed[k, at].astype(jnp.float32)
            total = total.astype(jnp.bfloat16)
            packed = jnp.zeros((wide, lay.piece), jnp.float32)
            for c in range(lay.cuts):
                packed += jnp.dot(pack_ref[c], total[:, c * lay.piece : (c + 1) * lay.piece],
                                  preferred_element_type=jnp.float32)
            sent[span(block, wide)] = packed.astype(jnp.bfloat16)

            @pl.loop(0, lay.merged)
            def _(j):
                owner = block * lay.merged + j

                @pl.when(owner != me)
                def _():
                    remote(sent.at[span(owner, lay.slab)], back.at[span(me, lay.slab)],
                           over_send.at[owner], over_recv.at[me], lay.peer(owner)).start()

        back[span(me, lay.slab)] = sent[span(me, lay.slab)]

        @pl.loop(1, lay.owners)
        def _(k):
            source = lax.rem(me + k, lay.owners)
            place = back.at[span(source, lay.slab)]
            remote(place, place, over_send.at[source], over_recv.at[source],
                   lay.peer(source)).wait_recv()

        for c in range(lay.cuts):
            o_ref[:, span(group, lay.share, c, lay.piece)] = jnp.dot(
                take_ref[c], back[...], preferred_element_type=jnp.float32
            ).astype(jnp.bfloat16)
        mine = o_ref.at[:, span(group, lay.share)]
        for k in range(lay.groups - 1):
            remote(mine, mine, across_send.at[k], across_recv.at[k], {"group": rest[k]}).start()
        for k in range(lay.groups - 1):
            origin = lax.rem(group + lay.groups - k - 1, lay.groups)
            place = o_ref.at[:, span(origin, lay.share)]
            remote(place, place, across_send.at[k], across_recv.at[k], {"group": rest[k]}).wait_recv()
        for k in range(lay.groups - 1):
            remote(mine, mine, across_send.at[k], across_recv.at[k], {"group": rest[k]}).wait_send()
            for b in range(lay.blocks):
                summing(b, k).wait_send()

        @pl.loop(1, lay.owners)
        def _(k):
            owner = lax.rem(me + k, lay.owners)
            place = sent.at[span(owner, lay.slab)]
            remote(place, place, over_send.at[owner], over_recv.at[owner], lay.peer(owner)).wait_send()

    dma = pltpu.SemaphoreType.DMA
    b16 = jnp.bfloat16
    return comm_call(
        kernel, jax.ShapeDtypeStruct((rows, lay.width), b16),
        [pltpu.VMEM((others, lay.owners * lay.slots, lay.share), b16),
         pltpu.VMEM((lay.owners * lay.slab, lay.piece), b16),
         pltpu.VMEM((lay.owners * lay.slab, lay.piece), b16),
         dma((others, lay.blocks)), dma((others, lay.blocks)),
         dma((lay.owners,)), dma((lay.owners,)), dma((others,)), dma((others,))],
        collective_id, partial, lay.pack, takes,
    )


def body(
    tokens, grad_out, w_qkv, w_attn_out, gain_attn, gain_ffn, w_gate_up, w_down, expert_ids, gates
):
    row_count, width = tokens.shape
    seq_len = row_count * lax.axis_size("head")
    head_cols = w_qkv.shape[2]
    head_count = head_cols // HD
    tokens_f = tokens.astype(jnp.float32)
    scale_one = inverse_rms(tokens_f)
    normed_one = (tokens_f * scale_one * gain_attn).astype(jnp.bfloat16)
    top_count = expert_ids.shape[1]
    owners = lax.axis_size(("dp", "head"))
    local_count = w_gate_up.shape[0]
    expert_count = local_count * owners
    capacity = max(row_count * top_count * 5 // (4 * expert_count), 2)
    flat_ids = expert_ids.reshape(-1)
    onehot = (flat_ids[:, None] == lax.iota(jnp.int32, expert_count)[None, :]).astype(jnp.int32)
    earlier = jnp.cumsum(onehot, axis=0) - onehot
    slot_ids = jnp.sum(onehot * earlier, axis=1)
    slots = local_count * capacity
    lay = Layout(slots, width)
    owner_ids = flat_ids // local_count
    places = owner_ids * lay.slab + (flat_ids % local_count) * capacity + slot_ids
    slab_rows = owners * lay.slab
    row_ids = lax.iota(jnp.int32, slab_rows)
    cut_ids = row_ids % lay.slab // lay.padded
    plain_ids = row_ids - cut_ids * lay.padded
    places = places.reshape(row_count, top_count)
    matches = plain_ids[:, None, None] == places[None]
    row_gates = jnp.sum(jnp.where(matches, gates[None], 0.0), axis=(1, 2))[:, None]
    cuts = lax.iota(jnp.int32, lay.cuts)
    picks = (
        jnp.any(matches, axis=2)[None] & (cut_ids[None, :] == cuts[:, None])[:, :, None]
    ).astype(jnp.bfloat16)
    takes = (
        jnp.any(places[:, :, None] == plain_ids[None, None, :], axis=1)[None]
        & (cut_ids[None, :] == cuts[:, None])[:, None, :]
    ).astype(jnp.bfloat16)
    shard_rows, got_grads = gather_head(normed_one, 0, Routed(lay, grad_out, picks, row_gates))
    fresh = jnp.einsum("rd,idh->irh", shard_rows, w_qkv, preferred_element_type=jnp.float32).astype(
        jnp.bfloat16
    )
    projected = fresh
    gathered = shard_rows
    projected, normed_all = (projected, gathered)
    split_heads = projected.reshape(3, seq_len, head_count, HD)
    query_heads = split_heads[0]
    key_heads = split_heads[1]
    value_heads = split_heads[2]
    chances = attention_probs(query_heads, key_heads)
    weights_b = chances.astype(jnp.bfloat16)
    mixed = (
        jnp.einsum("hqk,khd->qhd", weights_b, value_heads, preferred_element_type=jnp.float32)
        .astype(jnp.bfloat16)
        .reshape(seq_len, head_cols)
    )
    attn_sum = sum_to_rows(
        jnp.dot(mixed, w_attn_out, preferred_element_type=jnp.float32).astype(jnp.bfloat16), 1
    )
    hidden = (tokens_f + attn_sum).astype(jnp.bfloat16)
    hidden_f = hidden.astype(jnp.float32)
    scale_two = inverse_rms(hidden_f)
    normed_two = (hidden_f * scale_two * gain_ffn).astype(jnp.bfloat16)
    grad_f = grad_out.astype(jnp.float32)
    got_rows = route(Routed(lay, normed_two, picks), 2)

    def by_expert(got):
        got = got.reshape(owners, local_count, capacity, width)
        return jnp.swapaxes(got, 0, 1).reshape(local_count, owners * capacity, width)

    got_rows, got_grads = by_expert(got_rows), by_expert(got_grads)
    grad_pair, grad_down, returned = expert_work(got_rows, got_grads, w_gate_up, w_down)
    returned = returned.astype(jnp.bfloat16).reshape(local_count, owners, capacity, width)
    returned = jnp.swapaxes(returned, 0, 1).reshape(owners * slots, width)
    grad_normed = route_back(lay, returned, takes, 3).astype(jnp.float32)
    grad_hidden = grad_f + norm_backward(hidden_f, scale_two, gain_ffn, grad_normed)
    grad_hidden_b = grad_hidden.astype(jnp.bfloat16)
    shard_rows = gather_head_split(grad_hidden_b, 4)
    weight_total = jnp.einsum("rh,rd->dh", mixed, shard_rows, preferred_element_type=jnp.float32)
    fresh = jnp.einsum(
        "rd,hd->rh", shard_rows, w_attn_out, preferred_element_type=jnp.float32
    ).astype(jnp.bfloat16)
    grad_mixed = fresh
    grad_out_w, grad_mixed = (weight_total, grad_mixed)
    grad_heads = grad_mixed.reshape(seq_len, head_count, HD)
    grad_weights = jnp.einsum(
        "qhd,khd->hqk", grad_heads, value_heads, preferred_element_type=jnp.float32
    )
    grad_values = jnp.einsum(
        "hqk,qhd->khd", weights_b, grad_heads, preferred_element_type=jnp.float32
    ).astype(jnp.bfloat16)
    row_total = jnp.sum(chances * grad_weights, axis=-1, keepdims=True)
    grad_scores = (chances * (grad_weights - row_total) * HD ** (-0.5)).astype(jnp.bfloat16)
    grad_queries = jnp.einsum(
        "hqk,khd->qhd", grad_scores, key_heads, preferred_element_type=jnp.float32
    ).astype(jnp.bfloat16)
    grad_keys = jnp.einsum(
        "hqk,qhd->khd", grad_scores, query_heads, preferred_element_type=jnp.float32
    ).astype(jnp.bfloat16)
    grad_acts = jnp.stack([grad_queries, grad_keys, grad_values]).reshape(3, seq_len, head_cols)
    grad_proj = jnp.einsum("sd,ish->idh", normed_all, grad_acts, preferred_element_type=jnp.float32)
    grad_normed_one = sum_to_rows(
        jnp.einsum("irh,idh->rd", grad_acts, w_qkv, preferred_element_type=jnp.float32).astype(
            jnp.bfloat16
        ),
        5,
    )
    weight_grads = jnp.concatenate(
        [grad_proj.astype(jnp.bfloat16), grad_out_w.astype(jnp.bfloat16)[None]], axis=0
    )
    summed = lax.psum_scatter(weight_grads, "dp", scatter_dimension=1, tiled=True)
    grad_proj_sum = summed[:-1].astype(jnp.float32)
    grad_out_sum = summed[-1].T.astype(jnp.float32)
    grad_tokens = (
        grad_hidden + norm_backward(tokens_f, scale_one, gain_attn, grad_normed_one)
    ).astype(jnp.bfloat16)
    return (grad_tokens, grad_proj_sum, grad_out_sum, grad_pair, grad_down)


def solution(mesh):
    return jax.shard_map(
        body,
        mesh=mesh,
        in_specs=(
            P(("dp", "head"), None),
            P(("dp", "head"), None),
            P(None, None, ("head", "group")),
            P(("head", "group"), None),
            P(),
            P(),
            P(("dp", "head"), None, None, "group"),
            P(("dp", "head"), "group", None),
            P(("dp", "head"), None),
            P(("dp", "head"), None),
        ),
        out_specs=(
            P(("dp", "head"), None),
            P(None, "dp", ("head", "group")),
            P(("head", "group"), "dp"),
            P(("dp", "head"), None, None, "group"),
            P(("dp", "head"), "group", None),
        ),
        check_vma=False,
    )
```
